256 devices in a mesh: vocab: 32 (over y, x, core), dp: 8 (over z).
Axes of the slice: x: 4, y: 4, z: 8, core: 2. Of those that a mesh axis runs over, the one named last changes fastest.
Arguments:
- hidden: bfloat16 [1024, 4096], P('vocab', 'dp'), may hold values from -6 to 6
- head_weight: bfloat16 [4096, 65536], P('dp', 'vocab'), may hold values from -0.09375 to 0.09375
- grad_pooled: float32 [16, 65536], P(None, 'vocab'), may hold values from -6 to 6
- lengths: int32 [16], replicated, may hold values from 32 to 96, as said below
- argmax_local: int32 [16, 65536], P(None, 'vocab'), may hold values from 0 to 95, as said below
Outputs:
- grad_hidden: bfloat16 [1024, 4096], P('vocab', 'dp')
- grad_weight: bfloat16 [4096, 65536], P('dp', 'vocab')
The draws below stay inside these ranges and needn't reach their ends.
Inputs may be any that keep to these rules, and one draw needn't show every extreme that they name: The lengths sum to 1024. argmax_local[p, v] is less than lengths[p].
All inputs are finite; a program needn't handle non-finite values.
Results may differ from the reference program's by a relative error of at most 0.02.
Values may be sent and summed in bfloat16 or wider, within the bound.
A program may use at most 64 MiB of HBM per device.

```python
import jax
import jax.numpy as jnp
from jax import lax

D = 4096
TOK_DEV = 128
V = 65536
TOKENS = 1024
PASSAGES = 16


def passage_lengths(key):
    middle = TOK_DEV // 2
    reach = TOK_DEV // 4
    level_key = jax.random.fold_in(key, 13)
    rotate_key = jax.random.fold_in(key, 11)
    levels = jax.random.randint(level_key, (PASSAGES,), 0, reach + 1, dtype=jnp.int32)
    levels = levels.at[0].set(reach)
    levels = levels.at[1].set(jnp.maximum(levels[1], 1))
    levels = levels.at[2].set(reach)
    levels = levels.at[3].set(0)
    levels = levels.at[4].set(0)
    levels = levels.at[PASSAGES - 1].set(0)
    earlier = jnp.roll(levels, 1)
    spans = middle + levels - earlier
    rotate = jax.random.randint(rotate_key, (), 0, PASSAGES, dtype=jnp.int32)
    order = (jnp.arange(PASSAGES, dtype=jnp.int32) - rotate) % PASSAGES
    return spans[order].astype(jnp.int32)


def draw_lengths(key, part):
    return passage_lengths(key)


def draw_argmax_local(key, part):
    spans = passage_lengths(key)
    key = jax.random.fold_in(key, 7)
    values = jax.random.randint(key, (PASSAGES, V), 0, spans[:, None], dtype=jnp.int32)
    values = values.at[:, 0].set(spans - 1)
    values = values.at[:, 1].set(0)
    return values.astype(jnp.int32)


def level_of(own_key, extent, split, least, high):
    level = 1.0
    for axis_at, parts in split:
        steps = jax.random.uniform(jax.random.fold_in(jax.random.fold_in(own_key, 6), axis_at), (parts,), jnp.float32, least / len(split), high / len(split))
        level = level * jnp.repeat(jnp.exp(steps), extent[axis_at] // parts).reshape((-1,) + (1,) * (len(extent) - 1 - axis_at))
    return level


def normal_values(stream_key, shape, spread, limit, split=(), kind=jnp.bfloat16):
    array = spread * jax.random.normal(stream_key, shape, jnp.float32)
    if split:
        array = array * level_of(stream_key, shape, split, -0.22, 0.18)
    return jnp.clip(array, -limit, limit).astype(kind)


def setup_inputs(seed: int = 0) -> dict:
    seeds = jax.random.split(jax.random.key(seed), 6)
    hidden = normal_values(seeds[0], (TOKENS, D), 1.0, 6.0, ((0, 32), (1, 8)))
    head_weight = normal_values(seeds[1], (D, V), D ** -0.5, 0.09375, ((0, 8), (1, 32)))
    grad_pooled = normal_values(seeds[2], (PASSAGES, V), 1.0, 6.0, ((1, 32),), jnp.float32)
    lengths = draw_lengths(jax.random.fold_in(seeds[5], 71), 0)
    argmax_local = draw_argmax_local(jax.random.fold_in(seeds[5], 71), 0)
    return {"hidden": hidden, "head_weight": head_weight, "grad_pooled": grad_pooled, "lengths": lengths, "argmax_local": argmax_local}


flops_weight = 3.0


def reference(hidden, head_weight, grad_pooled, lengths, argmax_local):
    logits = jnp.dot(hidden, head_weight, preferred_element_type=jnp.float32)
    offsets = (jnp.cumsum(lengths) - lengths).astype(jnp.int32)
    hit = (offsets[:, None] + argmax_local).astype(jnp.int32)
    picked = jnp.take_along_axis(logits, hit, axis=0)
    soft = jax.nn.softplus(picked)
    pooled = jnp.log1p(soft)
    column = jnp.sum(pooled, axis=0)
    upstream = grad_pooled + (2.0 * flops_weight / (PASSAGES * PASSAGES)) * column[None, :]
    slope = upstream * jax.nn.sigmoid(picked) / (1.0 + soft)
    columns = lax.broadcasted_iota(jnp.int32, hit.shape, 1)
    dlogits = jnp.zeros((TOKENS, V), jnp.float32).at[hit, columns].add(slope).astype(jnp.bfloat16)
    grad_weight = lax.dot_general(hidden, dlogits, (((0,), (0,)), ((), ())), preferred_element_type=jnp.float32)
    grad_hidden = lax.dot_general(dlogits, head_weight, (((1,), (1,)), ((), ())), preferred_element_type=jnp.float32)
    return grad_hidden.astype(jnp.bfloat16), grad_weight.astype(jnp.bfloat16)
```

```python
import jax
import jax.numpy as jnp
from jax import lax
from jax.sharding import PartitionSpec as P

flops_weight = 3.0


def per_device(hidden, head_weight, grad_pooled, lengths, argmax_local):
    rows = lax.all_gather(hidden, "vocab", axis=0, tiled=True)
    tokens, passages = rows.shape[0], lengths.shape[0]
    ends = jnp.cumsum(lengths)
    starts = ends - lengths
    token = lax.broadcasted_iota(jnp.int32, (tokens, passages), 0)
    member = ((token >= starts[None, :]) & (token < ends[None, :])).astype(jnp.bfloat16)
    spread = jnp.dot(member, argmax_local.astype(jnp.bfloat16), preferred_element_type=jnp.float32)
    place = jnp.sum(jnp.where(member > 0, token - starts[None, :], 0), axis=1)
    matches = spread == place[:, None].astype(jnp.float32)
    logits = jnp.dot(rows, head_weight, preferred_element_type=jnp.float32)
    chosen = jnp.where(matches, logits, 0.0).astype(jnp.bfloat16)
    part = lax.dot_general(member, chosen, (((0,), (0,)), ((), ())), preferred_element_type=jnp.float32)
    picked = lax.psum(part.astype(jnp.bfloat16), "dp").astype(jnp.float32)
    soft = jax.nn.softplus(picked)
    column = jnp.sum(jnp.log1p(soft), axis=0)
    upstream = grad_pooled + 2.0 * flops_weight / (passages * passages) * column[None, :]
    slope = upstream * jax.nn.sigmoid(picked) / (1.0 + soft)
    wide = jnp.dot(member, slope.astype(jnp.bfloat16), preferred_element_type=jnp.float32)
    dlogits = jnp.where(matches, wide, 0.0).astype(jnp.bfloat16)
    hidden_part = lax.dot_general(
        dlogits, head_weight, (((1,), (1,)), ((), ())), preferred_element_type=jnp.float32
    )
    grad_hidden = lax.psum_scatter(hidden_part.astype(jnp.bfloat16), "vocab", scatter_dimension=0, tiled=True)
    grad_weight = lax.dot_general(
        rows, dlogits, (((0,), (0,)), ((), ())), preferred_element_type=jnp.float32
    )
    return (grad_hidden, grad_weight.astype(jnp.bfloat16))


def solution(mesh):
    in_specs = (P("vocab", "dp"), P("dp", "vocab"), P(None, "vocab"), P(), P(None, "vocab"))
    out_specs = (P("vocab", "dp"), P("dp", "vocab"))
    return jax.shard_map(
        per_device, mesh=mesh, in_specs=in_specs, out_specs=out_specs, check_vma=False
    )
```

```python
import functools

import jax
import jax.numpy as jnp
from jax import lax
from jax.experimental import pallas as pl
from jax.experimental.pallas import tpu as pltpu
from jax.sharding import PartitionSpec as P

flops_weight = 3.0
MESH = pl.DeviceIdType.MESH
f32, bf16 = jnp.float32, jnp.bfloat16
CUT = 4


def kernel(
    ny, nx, nz,
    len_ref, hid, w_hbm, gp_hbm, am_hbm,
    gh_ref, gw_hbm,
    rows, rows_t, w, w_t, mask, dl, am, gp, e, e_t, part, give, take, slopes,
    ghb, twin_in, rsend, rrecv, gwv,
    loc_sem, gw_sem, ag_s, ag_r, tw_s, tw_r, x1_s, x1_r, x2_s, x2_r, gt_s, gt_r, rs_s, rs_r,
):
    chips = ny * nx
    me, z = lax.axis_index("vocab"), lax.axis_index("dp")
    core, chip = lax.rem(me, 2), lax.div(me, 2)
    x, y = lax.rem(chip, nx), lax.div(chip, nx)
    twin = me + 1 - 2 * core
    tb, feats = hid.shape
    terms = w.shape[1]
    passages = len_ref.shape[0]
    group = nx * 2 * tb
    share = terms // nz
    wide = terms // CUT

    def to(src, dst, s, r, device):
        return pltpu.make_async_remote_copy(
            src_ref=src, dst_ref=dst, send_sem=s, recv_sem=r, device_id=device, device_id_type=MESH
        )

    local = [
        pltpu.make_async_copy(am_hbm, am, loc_sem.at[0]),
        pltpu.make_async_copy(hid, rows.at[y, x, core], loc_sem.at[1]),
        pltpu.make_async_copy(w_hbm, w, loc_sem.at[2]),
        pltpu.make_async_copy(gp_hbm.at[:, pl.ds(pl.multiple_of(z * share, share), share)], gp, loc_sem.at[3]),
    ]
    for copy in local:
        copy.start()

    barrier = pltpu.get_barrier_semaphore()
    for k in range(1, chips):
        pl.semaphore_signal(
            barrier, inc=1, device_id={"vocab": lax.rem(chip + k, chips) * 2 + core}, device_id_type=MESH
        )
    pl.semaphore_signal(barrier, inc=1, device_id={"vocab": twin}, device_id_type=MESH)
    for k in range(1, nz):
        pl.semaphore_signal(barrier, inc=1, device_id={"dp": lax.rem(z + k, nz)}, device_id_type=MESH)
    pl.semaphore_wait(barrier, chips + nz - 1)

    near = lambda n: sorted(range(n), key=lambda d: (min(d, n - d), d))
    offsets = [(dy, dx) for dy in near(ny) for dx in near(nx)]
    other = lambda dy, dx: (lax.rem(y + dy, ny), lax.rem(x + dx, nx))
    gather = []
    for dy, dx in offsets[1:]:
        oy, ox = other(dy, dx)
        at = oy * nx + ox
        copy = to(hid, rows.at[y, x, core], ag_s.at[at], ag_r.at[chip], {"vocab": at * 2 + core})
        copy.start()
        gather.append(copy)

    starts, begin = [], jnp.int32(0)
    for p in range(passages):
        starts.append(begin)
        begin = begin + len_ref[p]
    ends = starts[1:] + [begin]
    lane = lax.broadcasted_iota(jnp.int32, (group, passages), 1)
    first = jnp.zeros((group, passages), jnp.int32)
    last = jnp.zeros((group, passages), jnp.int32)
    sub = lax.broadcasted_iota(jnp.int32, (passages, group), 0)
    first_t = jnp.zeros((passages, group), jnp.int32)
    last_t = jnp.zeros((passages, group), jnp.int32)
    for p in range(passages):
        first = jnp.where(lane == p, starts[p], first)
        last = jnp.where(lane == p, ends[p], last)
        first_t = jnp.where(sub == p, starts[p], first_t)
        last_t = jnp.where(sub == p, ends[p], last_t)
    for g in range(ny):
        token = lax.broadcasted_iota(jnp.int32, (group, passages), 0) + g * group
        e[g] = jnp.where((token >= first) & (token < last), 1.0, 0.0).astype(bf16)
        token = lax.broadcasted_iota(jnp.int32, (passages, group), 1) + g * group
        e_t[g] = jnp.where((token >= first_t) & (token < last_t), 1.0, 0.0).astype(bf16)
    local[0].wait()

    def mark(g, carry):
        token = lax.broadcasted_iota(jnp.int32, (group, 1), 0) + g * group
        place = token
        for p in range(1, passages):
            place = jnp.where(token >= starts[p], token - starts[p], place)
        place = place.astype(f32)
        for n in range(CUT):
            cols = slice(n * wide, (n + 1) * wide)
            spread = jnp.dot(e[g], am[:, cols].astype(f32).astype(bf16), preferred_element_type=f32)
            mask[g, :, cols] = jnp.where(spread == place, 1.0, 0.0).astype(bf16)
        return carry

    lax.fori_loop(0, ny, mark, 0)
    local[1].wait()
    local[2].wait()

    def pick(g, start):
        block = rows[g].reshape(group, feats)
        for n in range(CUT):
            cols = slice(n * wide, (n + 1) * wide)
            logits = jnp.dot(block, w[:, cols], preferred_element_type=f32)
            chosen = logits.astype(bf16) * mask[g, :, cols]
            found = jnp.dot(e_t[g], chosen, preferred_element_type=f32)
            for j in range(wide // share):
                at = n * (wide // share) + j
                piece = found[:, j * share:(j + 1) * share]
                part[at] = piece if start else part[at] + piece

    forward = []
    for s, dy in enumerate(near(ny)):
        g = lax.rem(y + dy, ny)
        for dx in near(nx):
            if dy or dx:
                oy, ox = other(dy, dx)
                at = oy * nx + ox
                to(hid, rows.at[oy, ox, core], ag_s.at[at], ag_r.at[at], {"vocab": twin}).wait_recv()
        copy = to(rows.at[g, :, core], rows.at[g, :, core], tw_s.at[s], tw_r.at[s], {"vocab": twin})
        copy.start()
        forward.append(copy)
        if s:
            pick(lax.rem(y + near(ny)[s - 1], ny), s == 1)
        to(rows.at[g, :, 1 - core], rows.at[g, :, 1 - core], tw_s.at[s], tw_r.at[s], {"vocab": twin}).wait_recv()
    pick(lax.rem(y + near(ny)[-1], ny), ny == 1)

    for j in range(nz):
        give[j] = part[j].astype(bf16)
    ask = []
    for k in range(1, nz):
        oz = lax.rem(z + k, nz)
        copy = to(give.at[oz], take.at[z], x1_s.at[oz], x1_r.at[z], {"dp": oz})
        copy.start()
        ask.append(copy)
    take[z] = give[z]
    for g in range(ny):
        rows_t[:, g * group:(g + 1) * group] = rows[g].reshape(group, feats).T
    for k in range(1, nz):
        oz = lax.rem(z + k, nz)
        to(give.at[oz], take.at[oz], x1_s.at[oz], x1_r.at[oz], {"dp": oz}).wait_recv()
    local[3].wait()
    picked = take[0].astype(f32)
    for j in range(1, nz):
        picked = picked + take[j].astype(f32)
    small = jnp.exp(-jnp.abs(picked))
    soft = jnp.maximum(picked, 0.0) + jnp.log1p(small)
    column = jnp.sum(jnp.log1p(soft), axis=0, keepdims=True)
    upstream = gp[...] + 2.0 * flops_weight / (passages * passages) * column
    sigmoid = jnp.where(picked >= 0, 1.0, small) / (1.0 + small)
    slopes[z] = (upstream * sigmoid / (1.0 + soft)).astype(bf16)
    answer = []
    for k in range(1, nz):
        oz = lax.rem(z + k, nz)
        copy = to(slopes.at[z], slopes.at[z], x2_s.at[oz], x2_r.at[z], {"dp": oz})
        copy.start()
        answer.append(copy)
    for n in range(CUT):
        w_t[n * wide:(n + 1) * wide, :] = w[:, n * wide:(n + 1) * wide].T
    for k in range(1, nz):
        oz = lax.rem(z + k, nz)
        to(slopes.at[z], slopes.at[oz], x2_s.at[oz], x2_r.at[oz], {"dp": oz}).wait_recv()

    scatter, halves = [], []

    def send_on(s, dy):
        g = lax.rem(y + dy, ny)
        to(ghb.at[g, :, core], twin_in.at[g], gt_s.at[s], gt_r.at[s], {"vocab": twin}).wait_recv()
        rsend[g] = (twin_in[g].astype(f32) + ghb[g, :, core].astype(f32)).astype(bf16)
        for dx in near(nx):
            if dy or dx:
                oy, ox = other(dy, dx)
                at = oy * nx + ox
                copy = to(rsend.at[oy, ox], rrecv.at[chip], rs_s.at[at], rs_r.at[chip], {"vocab": at * 2 + core})
                copy.start()
                scatter.append(copy)

    far = near(ny)[::-1]
    for s, dy in enumerate(far):
        g = lax.rem(y + dy, ny)
        for n in range(CUT):
            cols = slice(n * wide, (n + 1) * wide)
            slope = jnp.concatenate([slopes[j] for j in range(n * nz // CUT, (n + 1) * nz // CUT)], axis=1)
            spread = jnp.dot(e[g], slope, preferred_element_type=f32)
            dl[g, :, cols] = spread.astype(bf16) * mask[g, :, cols]
        total = jnp.dot(dl[g], w_t[...], preferred_element_type=f32)
        ghb[g] = total.astype(bf16).reshape(nx, 2, tb, feats)
        copy = to(ghb.at[g, :, 1 - core], twin_in.at[g], gt_s.at[s], gt_r.at[s], {"vocab": twin})
        copy.start()
        halves.append(copy)
        if s:
            send_on(s - 1, far[s - 1])

    written = []
    for n in range(CUT):
        cols = slice(n * wide, (n + 1) * wide)
        block = dl[:, :, cols].reshape(ny * group, wide)
        gwv[:, cols] = jnp.dot(rows_t[...], block, preferred_element_type=f32).astype(bf16)
        copy = pltpu.make_async_copy(gwv.at[:, cols], gw_hbm.at[:, cols], gw_sem.at[n])
        copy.start()
        written.append(copy)
        if n == 0:
            send_on(ny - 1, far[-1])

    for dy, dx in offsets[1:]:
        oy, ox = other(dy, dx)
        at = oy * nx + ox
        to(rsend.at[oy, ox], rrecv.at[at], rs_s.at[at], rs_r.at[at], {"vocab": twin}).wait_recv()
    rrecv[chip] = rsend[y, x]
    total = rrecv[0].astype(f32)
    for k in range(1, chips):
        total = total + rrecv[k].astype(f32)
    gh_ref[...] = total.astype(bf16)
    for copy in gather + forward + ask + answer + halves + scatter:
        copy.wait_send()
    for copy in written:
        copy.wait()


def per_device(nx, nz, hidden, head_weight, grad_pooled, lengths, argmax_local):
    tb, feats = hidden.shape
    terms = head_weight.shape[1]
    passages = lengths.shape[0]
    chips = lax.axis_size("vocab") // 2
    ny = chips // nx
    group = nx * 2 * tb
    tokens = ny * group
    share = terms // nz
    anywhere = pl.BlockSpec(memory_space=pl.ANY)
    dma = pltpu.SemaphoreType.DMA
    return pl.pallas_call(
        functools.partial(kernel, ny, nx, nz),
        out_shape=(
            jax.ShapeDtypeStruct((tb, feats), bf16),
            jax.ShapeDtypeStruct((feats, terms), bf16),
        ),
        in_specs=[pl.BlockSpec(memory_space=pltpu.SMEM)] + [anywhere] * 4,
        out_specs=(pl.BlockSpec(memory_space=pltpu.VMEM), anywhere),
        scratch_shapes=[
            pltpu.VMEM((ny, nx, 2, tb, feats), bf16),
            pltpu.VMEM((feats, tokens), bf16),
            pltpu.VMEM((feats, terms), bf16),
            pltpu.VMEM((terms, feats), bf16),
            pltpu.VMEM((ny, group, terms), bf16),
            pltpu.VMEM((ny, group, terms), bf16),
            pltpu.VMEM((passages, terms), jnp.int32),
            pltpu.VMEM((passages, share), f32),
            pltpu.VMEM((ny, group, passages), bf16),
            pltpu.VMEM((ny, passages, group), bf16),
            pltpu.VMEM((nz, passages, share), f32),
            pltpu.VMEM((nz, passages, share), bf16),
            pltpu.VMEM((nz, passages, share), bf16),
            pltpu.VMEM((nz, passages, share), bf16),
            pltpu.VMEM((ny, nx, 2, tb, feats), bf16),
            pltpu.VMEM((ny, nx, tb, feats), bf16),
            pltpu.VMEM((ny, nx, tb, feats), bf16),
            pltpu.VMEM((chips, tb, feats), bf16),
            pltpu.VMEM((feats, terms), bf16),
            dma((4,)), dma((CUT,)),
            dma((chips,)), dma((chips,)),
            dma((ny,)), dma((ny,)),
            dma((nz,)), dma((nz,)),
            dma((nz,)), dma((nz,)),
            dma((ny,)), dma((ny,)),
            dma((chips,)), dma((chips,)),
        ],
        compiler_params=pltpu.CompilerParams(
            collective_id=0, has_side_effects=True, vmem_limit_bytes=56 * 1024 * 1024
        ),
        cost_estimate=pl.CostEstimate(
            flops=6 * tokens * feats * terms, bytes_accessed=4 * feats * terms, transcendentals=0
        ),
    )(lengths, hidden, head_weight, grad_pooled, argmax_local)


def solution(mesh):
    in_specs = (P("vocab", "dp"), P("dp", "vocab"), P(None, "vocab"), P(), P(None, "vocab"))
    out_specs = (P("vocab", "dp"), P("dp", "vocab"))
    nx = 4 if mesh.shape["vocab"] == 32 else 2
    return jax.shard_map(
        functools.partial(per_device, nx, mesh.shape["dp"]),
        mesh=mesh, in_specs=in_specs, out_specs=out_specs, check_vma=False,
    )
```

```python
import functools

import jax
import jax.numpy as jnp
from jax import lax
from jax.experimental import pallas as pl
from jax.experimental.pallas import tpu as pltpu
from jax.sharding import PartitionSpec as P

flops_weight = 3.0
MESH = pl.DeviceIdType.MESH
f32, bf16 = jnp.float32, jnp.bfloat16
CUT = 4


def kernel(
    ny, nx, nz,
    len_ref, hid, w_hbm, gp_hbm, am_hbm,
    gh, gw,
    rows, rows_t, w, w_t, mask, dl, am, gp, e, e_t, part, give, take, slopes,
    twin_out, twin_in, rsend, rrecv,
    loc_sem, ag_s, ag_r, tw_s, tw_r, x1_s, x1_r, x2_s, x2_r, gt_s, gt_r, rs_s, rs_r,
):
    chips = ny * nx
    me, z = lax.axis_index("vocab"), lax.axis_index("dp")
    core, chip = lax.rem(me, 2), lax.div(me, 2)
    x, y = lax.rem(chip, nx), lax.div(chip, nx)
    mate = 1 - core
    twin = chip * 2 + mate
    tb, feats = hid.shape
    terms = w.shape[1]
    passages = len_ref.shape[0]
    band = nx * tb
    share = terms // nz
    wide = terms // CUT

    def to(src, dst, s, r, device):
        return pltpu.make_async_remote_copy(
            src_ref=src, dst_ref=dst, send_sem=s, recv_sem=r, device_id=device, device_id_type=MESH
        )

    local = [
        pltpu.make_async_copy(hid, rows.at[core, y, x], loc_sem.at[0]),
        pltpu.make_async_copy(am_hbm, am, loc_sem.at[1]),
        pltpu.make_async_copy(w_hbm, w, loc_sem.at[2]),
        pltpu.make_async_copy(gp_hbm.at[:, pl.ds(pl.multiple_of(z * share, share), share)], gp, loc_sem.at[3]),
    ]
    for copy in local:
        copy.start()

    barrier = pltpu.get_barrier_semaphore()
    for k in range(1, chips):
        pl.semaphore_signal(
            barrier, inc=1, device_id={"vocab": lax.rem(chip + k, chips) * 2 + core}, device_id_type=MESH
        )
    pl.semaphore_signal(barrier, inc=1, device_id={"vocab": twin}, device_id_type=MESH)
    for k in range(1, nz):
        pl.semaphore_signal(barrier, inc=1, device_id={"dp": lax.rem(z + k, nz)}, device_id_type=MESH)

    local[0].wait()
    pl.semaphore_wait(barrier, chips + nz - 1)

    near = lambda n: sorted(range(n), key=lambda d: (min(d, n - d), d))
    offsets = [(dy, dx) for dy in near(ny) for dx in near(nx)]
    other = lambda dy, dx: (lax.rem(y + dy, ny), lax.rem(x + dx, nx))
    gather = []
    for dy, dx in sorted(offsets[1:], key=lambda o: -min(o[0], ny - o[0]) - min(o[1], nx - o[1])):
        oy, ox = other(dy, dx)
        at = oy * nx + ox
        copy = to(rows.at[core, y, x], rows.at[core, y, x], ag_s.at[at], ag_r.at[chip], {"vocab": at * 2 + core})
        copy.start()
        gather.append(copy)

    starts, begin = [], jnp.int32(0)
    for p in range(passages):
        starts.append(begin)
        begin = begin + len_ref[p]
    ends = starts[1:] + [begin]

    def tokens(shape, dim, c, g):
        i = lax.broadcasted_iota(jnp.int32, shape, dim)
        return i + jnp.bitwise_and(i, -tb) + (g * 2 * band + c * tb)

    lane = lax.broadcasted_iota(jnp.int32, (band, passages), 1)
    first = jnp.zeros((band, passages), jnp.int32)
    last = jnp.zeros((band, passages), jnp.int32)
    sub = lax.broadcasted_iota(jnp.int32, (passages, band), 0)
    first_t = jnp.zeros((passages, band), jnp.int32)
    last_t = jnp.zeros((passages, band), jnp.int32)
    for p in range(passages):
        first = jnp.where(lane == p, starts[p], first)
        last = jnp.where(lane == p, ends[p], last)
        first_t = jnp.where(sub == p, starts[p], first_t)
        last_t = jnp.where(sub == p, ends[p], last_t)
    for c in range(2):
        for g in range(ny):
            token = tokens((band, passages), 0, c, g)
            e[c, g] = jnp.where((token >= first) & (token < last), 1.0, 0.0).astype(bf16)
            token = tokens((passages, band), 1, c, g)
            e_t[c, g] = jnp.where((token >= first_t) & (token < last_t), 1.0, 0.0).astype(bf16)
    local[1].wait()

    def mark(c, carry):
        places = []
        for g in range(ny):
            token = tokens((band, 1), 0, c, g)
            place = token
            for p in range(1, passages):
                place = jnp.where(token >= starts[p], token - starts[p], place)
            places.append(place)
        place = jnp.concatenate(places, axis=0).astype(f32)
        member = e[c].reshape(ny * band, passages)
        for n in range(CUT):
            cols = slice(n * wide, (n + 1) * wide)
            spread = jnp.dot(member, am[:, cols].astype(f32).astype(bf16), preferred_element_type=f32)
            mask[c, :, :, cols] = jnp.where(spread == place, 1.0, 0.0).astype(bf16).reshape(ny, band, wide)
        return carry

    lax.fori_loop(0, 2, mark, 0)
    local[2].wait()
    for n in range(CUT):
        w_t[n * wide:(n + 1) * wide, :] = w[:, n * wide:(n + 1) * wide].T

    def pick(c, bands, start):
        block = jnp.concatenate([rows[c, g].reshape(band, feats) for g in bands], axis=0)
        member = jnp.concatenate([e_t[c, g] for g in bands], axis=1)
        logits = jnp.dot(block, w[...], preferred_element_type=f32)
        marks = jnp.concatenate([mask[c, g] for g in bands], axis=0)
        found = jnp.dot(member, logits.astype(bf16) * marks, preferred_element_type=f32)
        for j in range(nz):
            piece = found[:, j * share:(j + 1) * share]
            part[j] = piece if start else part[j] + piece

    near_y = near(ny)
    pairs = [near_y]
    forward = []
    for s, pair in enumerate(pairs):
        bands = [lax.rem(y + dy, ny) for dy in pair]
        for dy, g in zip(pair, bands):
            for dx in near(nx):
                if dy or dx:
                    oy, ox = other(dy, dx)
                    at = oy * nx + ox
                    to(rows.at[core, oy, ox], rows.at[core, oy, ox], ag_s.at[at], ag_r.at[at], {"vocab": twin}).wait_recv()
            copy = to(rows.at[core, g], rows.at[core, g], tw_s.at[dy], tw_r.at[dy], {"vocab": twin})
            copy.start()
            forward.append(copy)
        pick(core, bands, s == 0)
        for dy, g in zip(pair, bands):
            to(rows.at[mate, g], rows.at[mate, g], tw_s.at[dy], tw_r.at[dy], {"vocab": twin}).wait_recv()
        pick(mate, bands, False)

    for j in range(nz):
        give[j] = part[j].astype(bf16)
    ask = []
    for k in range(1, nz):
        oz = lax.rem(z + k, nz)
        copy = to(give.at[oz], take.at[z], x1_s.at[oz], x1_r.at[z], {"dp": oz})
        copy.start()
        ask.append(copy)
    take[z] = give[z]
    for c in range(2):
        rows_t[:, c * ny * band:(c + 1) * ny * band] = rows[c].reshape(ny * band, feats).T
    for k in range(1, nz):
        oz = lax.rem(z + k, nz)
        to(give.at[oz], take.at[oz], x1_s.at[oz], x1_r.at[oz], {"dp": oz}).wait_recv()
    local[3].wait()
    picked = take[0].astype(f32)
    for j in range(1, nz):
        picked = picked + take[j].astype(f32)
    small = jnp.exp(-jnp.abs(picked))
    soft = jnp.maximum(picked, 0.0) + jnp.log1p(small)
    column = jnp.sum(jnp.log1p(soft), axis=0, keepdims=True)
    upstream = gp[...] + 2.0 * flops_weight / (passages * passages) * column
    sigmoid = jnp.where(picked >= 0, 1.0, small) / (1.0 + small)
    slopes[z] = (upstream * sigmoid / (1.0 + soft)).astype(bf16)
    answer = []
    for k in range(1, nz):
        oz = lax.rem(z + k, nz)
        copy = to(slopes.at[z], slopes.at[z], x2_s.at[oz], x2_r.at[z], {"dp": oz})
        copy.start()
        answer.append(copy)
    for k in range(1, nz):
        oz = lax.rem(z + k, nz)
        to(slopes.at[z], slopes.at[oz], x2_s.at[oz], x2_r.at[oz], {"dp": oz}).wait_recv()

    def spread_slopes(c, bands):
        member = jnp.concatenate([e[c, g] for g in bands], axis=0)
        slope = jnp.concatenate([slopes[j] for j in range(nz)], axis=1)
        wider = jnp.dot(member, slope, preferred_element_type=f32).astype(bf16)
        for i, g in enumerate(bands):
            dl[c, g] = wider[i * band:(i + 1) * band] * mask[c, g]

    def hidden_part(c, bands):
        block = jnp.concatenate([dl[c, g] for g in bands], axis=0)
        return jnp.dot(block, w_t[...], preferred_element_type=f32)

    scatter, halves = [], []
    for pair in pairs[::-1]:
        bands = [lax.rem(y + dy, ny) for dy in pair]
        spread_slopes(mate, bands)
        total = hidden_part(mate, bands).astype(bf16)
        for i, (dy, g) in enumerate(zip(pair, bands)):
            twin_out[dy] = total[i * band:(i + 1) * band]
            copy = to(twin_out.at[dy], twin_in.at[dy], gt_s.at[dy], gt_r.at[dy], {"vocab": twin})
            copy.start()
            halves.append(copy)
        spread_slopes(core, bands)
        total = hidden_part(core, bands)
        for i, (dy, g) in enumerate(zip(pair, bands)):
            to(twin_out.at[dy], twin_in.at[dy], gt_s.at[dy], gt_r.at[dy], {"vocab": twin}).wait_recv()
            both = total[i * band:(i + 1) * band] + twin_in[dy].astype(f32)
            rsend[g] = both.astype(bf16).reshape(nx, tb, feats)
            for dx in near(nx)[::-1]:
                if dy or dx:
                    oy, ox = other(dy, dx)
                    at = oy * nx + ox
                    copy = to(rsend.at[oy, ox], rrecv.at[chip], rs_s.at[at], rs_r.at[chip], {"vocab": at * 2 + core})
                    copy.start()
                    scatter.append(copy)

    block = dl[...].reshape(2 * ny * band, terms)
    gw[...] = jnp.dot(rows_t[...], block, preferred_element_type=f32).astype(bf16)

    rrecv[chip] = rsend[y, x]
    for dy, dx in offsets[1:]:
        oy, ox = other(dy, dx)
        at = oy * nx + ox
        to(rsend.at[oy, ox], rrecv.at[at], rs_s.at[at], rs_r.at[at], {"vocab": twin}).wait_recv()
    total = rrecv[0].astype(f32)
    for k in range(1, chips):
        total = total + rrecv[k].astype(f32)
    gh[...] = total.astype(bf16)
    for copy in gather + forward + ask + answer + halves + scatter:
        copy.wait_send()


def per_device(nx, nz, hidden, head_weight, grad_pooled, lengths, argmax_local):
    tb, feats = hidden.shape
    terms = head_weight.shape[1]
    passages = lengths.shape[0]
    chips = lax.axis_size("vocab") // 2
    ny = chips // nx
    band = nx * tb
    tokens = 2 * ny * band
    share = terms // nz
    anywhere = pl.BlockSpec(memory_space=pl.ANY)
    dma = pltpu.SemaphoreType.DMA
    return pl.pallas_call(
        functools.partial(kernel, ny, nx, nz),
        out_shape=(pltpu.VMEM((tb, feats), bf16), pltpu.VMEM((feats, terms), bf16)),
        in_specs=[pl.BlockSpec(memory_space=pltpu.SMEM)] + [anywhere] * 4,
        out_specs=(pl.BlockSpec(memory_space=pltpu.VMEM), pl.BlockSpec(memory_space=pltpu.VMEM)),
        scratch_shapes=[
            pltpu.VMEM((2, ny, nx, tb, feats), bf16),
            pltpu.VMEM((feats, tokens), bf16),
            pltpu.VMEM((feats, terms), bf16),
            pltpu.VMEM((terms, feats), bf16),
            pltpu.VMEM((2, ny, band, terms), bf16),
            pltpu.VMEM((2, ny, band, terms), bf16),
            pltpu.VMEM((passages, terms), jnp.int32),
            pltpu.VMEM((passages, share), f32),
            pltpu.VMEM((2, ny, band, passages), bf16),
            pltpu.VMEM((2, ny, passages, band), bf16),
            pltpu.VMEM((nz, passages, share), f32),
            pltpu.VMEM((nz, passages, share), bf16),
            pltpu.VMEM((nz, passages, share), bf16),
            pltpu.VMEM((nz, passages, share), bf16),
            pltpu.VMEM((ny, band, feats), bf16),
            pltpu.VMEM((ny, band, feats), bf16),
            pltpu.VMEM((ny, nx, tb, feats), bf16),
            pltpu.VMEM((chips, tb, feats), bf16),
            dma((4,)),
            dma((chips,)), dma((chips,)),
            dma((ny,)), dma((ny,)),
            dma((nz,)), dma((nz,)),
            dma((nz,)), dma((nz,)),
            dma((ny,)), dma((ny,)),
            dma((chips,)), dma((chips,)),
        ],
        compiler_params=pltpu.CompilerParams(
            collective_id=0, has_side_effects=True, vmem_limit_bytes=56 * 1024 * 1024
        ),
        cost_estimate=pl.CostEstimate(
            flops=6 * tokens * feats * terms, bytes_accessed=4 * feats * terms, transcendentals=0
        ),
    )(lengths, hidden, head_weight, grad_pooled, argmax_local)


def solution(mesh):
    in_specs = (P("vocab", "dp"), P("dp", "vocab"), P(None, "vocab"), P(), P(None, "vocab"))
    out_specs = (P("vocab", "dp"), P("dp", "vocab"))
    nx = 4 if mesh.shape["vocab"] == 32 else 2
    return jax.shard_map(
        functools.partial(per_device, nx, mesh.shape["dp"]),
        mesh=mesh, in_specs=in_specs, out_specs=out_specs, check_vma=False,
    )
```

```python
import functools

import jax
import jax.numpy as jnp
from jax import lax
from jax.experimental import pallas as pl
from jax.experimental.pallas import tpu as pltpu
from jax.sharding import PartitionSpec as P

flops_weight = 3.0
MESH = pl.DeviceIdType.MESH
f32, bf16 = jnp.float32, jnp.bfloat16
CUT = 4


def kernel(
    ny, nx, nz,
    len_ref, hid, w_hbm, gp_hbm, am_hbm,
    gh, gw,
    rows, rows_t, w, w_t, mask, dl, am, gp, e, e_t, part, give, take, slopes,
    twin_out, twin_in, rsend, rrecv,
    loc_sem, ag_s, ag_r, tw_s, tw_r, x1_s, x1_r, x2_s, x2_r, gt_s, gt_r, rs_s, rs_r,
):
    chips = ny * nx
    me, z = lax.axis_index("vocab"), lax.axis_index("dp")
    core, chip = lax.rem(me, 2), lax.div(me, 2)
    x, y = lax.rem(chip, nx), lax.div(chip, nx)
    mate = 1 - core
    twin = chip * 2 + mate
    tb, feats = hid.shape
    terms = w.shape[1]
    passages = len_ref.shape[0]
    band = nx * tb
    share = terms // nz
    wide = terms // CUT

    def to(src, dst, s, r, device):
        return pltpu.make_async_remote_copy(
            src_ref=src, dst_ref=dst, send_sem=s, recv_sem=r, device_id=device, device_id_type=MESH
        )

    local = [
        pltpu.make_async_copy(hid, rows.at[core, y, x], loc_sem.at[0]),
        pltpu.make_async_copy(am_hbm, am, loc_sem.at[1]),
        pltpu.make_async_copy(w_hbm, w, loc_sem.at[2]),
        pltpu.make_async_copy(gp_hbm.at[:, pl.ds(pl.multiple_of(z * share, share), share)], gp, loc_sem.at[3]),
    ]
    for copy in local:
        copy.start()

    near = lambda n: sorted(range(n), key=lambda d: (min(d, n - d), d))
    offsets = [(dy, dx) for dy in near(ny) for dx in near(nx)]
    far_xy = sorted(offsets[1:], key=lambda o: -min(o[0], ny - o[0]) - min(o[1], nx - o[1]))
    far_z = near(nz)[:0:-1]
    other = lambda dy, dx: (lax.rem(y + dy, ny), lax.rem(x + dx, nx))

    barrier = pltpu.get_barrier_semaphore()
    for dy, dx in far_xy:
        oy, ox = other(dy, dx)
        pl.semaphore_signal(barrier, inc=1, device_id={"vocab": (oy * nx + ox) * 2 + core}, device_id_type=MESH)
    pl.semaphore_signal(barrier, inc=1, device_id={"vocab": twin}, device_id_type=MESH)
    for k in far_z:
        pl.semaphore_signal(barrier, inc=1, device_id={"dp": lax.rem(z + k, nz)}, device_id_type=MESH)

    local[0].wait()
    pl.semaphore_wait(barrier, chips + nz - 1)

    gather = []
    for dy, dx in far_xy:
        oy, ox = other(dy, dx)
        at = oy * nx + ox
        copy = to(rows.at[core, y, x], rows.at[core, y, x], ag_s.at[at], ag_r.at[chip], {"vocab": at * 2 + core})
        copy.start()
        gather.append(copy)

    starts, begin = [], jnp.int32(0)
    for p in range(passages):
        starts.append(begin)
        begin = begin + len_ref[p]
    ends = starts[1:] + [begin]

    def tokens(shape, dim, c, g):
        i = lax.broadcasted_iota(jnp.int32, shape, dim)
        return i + jnp.bitwise_and(i, -tb) + (g * 2 * band + c * tb)

    lane = lax.broadcasted_iota(jnp.int32, (band, passages), 1)
    first = jnp.zeros((band, passages), jnp.int32)
    last = jnp.zeros((band, passages), jnp.int32)
    sub = lax.broadcasted_iota(jnp.int32, (passages, band), 0)
    first_t = jnp.zeros((passages, band), jnp.int32)
    last_t = jnp.zeros((passages, band), jnp.int32)
    for p in range(passages):
        first = jnp.where(lane == p, starts[p], first)
        last = jnp.where(lane == p, ends[p], last)
        first_t = jnp.where(sub == p, starts[p], first_t)
        last_t = jnp.where(sub == p, ends[p], last_t)
    for c in range(2):
        for g in range(ny):
            token = tokens((band, passages), 0, c, g)
            e[c, g] = jnp.where((token >= first) & (token < last), 1.0, 0.0).astype(bf16)
            token = tokens((passages, band), 1, c, g)
            e_t[c, g] = jnp.where((token >= first_t) & (token < last_t), 1.0, 0.0).astype(bf16)
    local[1].wait()

    def mark(c, carry):
        places = []
        for g in range(ny):
            token = tokens((band, 1), 0, c, g)
            place = token
            for p in range(1, passages):
                place = jnp.where(token >= starts[p], token - starts[p], place)
            places.append(place)
        place = jnp.concatenate(places, axis=0).astype(f32)
        member = e[c].reshape(ny * band, passages)
        for n in range(CUT):
            cols = slice(n * wide, (n + 1) * wide)
            spread = jnp.dot(member, am[:, cols].astype(f32).astype(bf16), preferred_element_type=f32)
            mask[c, :, :, cols] = jnp.where(spread == place, 1.0, 0.0).astype(bf16).reshape(ny, band, wide)
        return carry

    lax.fori_loop(0, 2, mark, 0)
    local[2].wait()
    for n in range(CUT):
        w_t[n * wide:(n + 1) * wide, :] = w[:, n * wide:(n + 1) * wide].T

    def pick(c, bands, start):
        block = jnp.concatenate([rows[c, g].reshape(band, feats) for g in bands], axis=0)
        member = jnp.concatenate([e_t[c, g] for g in bands], axis=1)
        logits = jnp.dot(block, w[...], preferred_element_type=f32)
        marks = jnp.concatenate([mask[c, g] for g in bands], axis=0)
        found = jnp.dot(member, logits.astype(bf16) * marks, preferred_element_type=f32)
        for j in range(nz):
            piece = found[:, j * share:(j + 1) * share]
            part[j] = piece if start else part[j] + piece

    near_y = near(ny)
    pairs = [near_y[::-1][:ny // 2], near_y[::-1][ny // 2:]]
    parts = [near_y[::-1][:ny // 2], near_y[::-1][ny // 2:]]
    forward = []
    for s, pair in enumerate(pairs):
        bands = [lax.rem(y + dy, ny) for dy in pair]
        for dy, g in zip(pair, bands):
            for dx in near(nx):
                if dy or dx:
                    oy, ox = other(dy, dx)
                    at = oy * nx + ox
                    to(rows.at[core, oy, ox], rows.at[core, oy, ox], ag_s.at[at], ag_r.at[at], {"vocab": twin}).wait_recv()
            copy = to(rows.at[core, g], rows.at[core, g], tw_s.at[dy], tw_r.at[dy], {"vocab": twin})
            copy.start()
            forward.append(copy)
        pick(core, bands, s == 0)
        for dy, g in zip(pair, bands):
            to(rows.at[mate, g], rows.at[mate, g], tw_s.at[dy], tw_r.at[dy], {"vocab": twin}).wait_recv()
        pick(mate, bands, False)

    for j in range(nz):
        give[j] = part[j].astype(bf16)
    ask = []
    for k in far_z:
        oz = lax.rem(z + k, nz)
        copy = to(give.at[oz], take.at[z], x1_s.at[oz], x1_r.at[z], {"dp": oz})
        copy.start()
        ask.append(copy)
    take[z] = give[z]
    for c in range(2):
        rows_t[:, c * ny * band:(c + 1) * ny * band] = rows[c].reshape(ny * band, feats).T
    for k in far_z:
        oz = lax.rem(z + k, nz)
        to(give.at[oz], take.at[oz], x1_s.at[oz], x1_r.at[oz], {"dp": oz}).wait_recv()
    local[3].wait()
    picked = take[0].astype(f32)
    for j in range(1, nz):
        picked = picked + take[j].astype(f32)
    small = jnp.exp(-jnp.abs(picked))
    soft = jnp.maximum(picked, 0.0) + jnp.log1p(small)
    column = jnp.sum(jnp.log1p(soft), axis=0, keepdims=True)
    upstream = gp[...] + 2.0 * flops_weight / (passages * passages) * column
    sigmoid = jnp.where(picked >= 0, 1.0, small) / (1.0 + small)
    slopes[z] = (upstream * sigmoid / (1.0 + soft)).astype(bf16)
    answer = []
    for k in far_z:
        oz = lax.rem(z + k, nz)
        copy = to(slopes.at[z], slopes.at[z], x2_s.at[oz], x2_r.at[z], {"dp": oz})
        copy.start()
        answer.append(copy)
    for k in far_z:
        oz = lax.rem(z + k, nz)
        to(slopes.at[z], slopes.at[oz], x2_s.at[oz], x2_r.at[oz], {"dp": oz}).wait_recv()

    def spread_slopes(c, bands):
        member = jnp.concatenate([e[c, g] for g in bands], axis=0)
        slope = jnp.concatenate([slopes[j] for j in range(nz)], axis=1)
        wider = jnp.dot(member, slope, preferred_element_type=f32).astype(bf16)
        for i, g in enumerate(bands):
            dl[c, g] = wider[i * band:(i + 1) * band] * mask[c, g]

    def hidden_part(c, bands):
        block = jnp.concatenate([dl[c, g] for g in bands], axis=0)
        return jnp.dot(block, w_t[...], preferred_element_type=f32)

    scatter, halves = [], []
    for pair in parts:
        bands = [lax.rem(y + dy, ny) for dy in pair]
        spread_slopes(mate, bands)
        total = hidden_part(mate, bands).astype(bf16)
        for i, dy in enumerate(pair):
            twin_out[dy] = total[i * band:(i + 1) * band]
            copy = to(twin_out.at[dy], twin_in.at[dy], gt_s.at[dy], gt_r.at[dy], {"vocab": twin})
            copy.start()
            halves.append(copy)
    for pair in parts:
        bands = [lax.rem(y + dy, ny) for dy in pair]
        spread_slopes(core, bands)
        total = hidden_part(core, bands)
        for i, (dy, g) in enumerate(zip(pair, bands)):
            to(twin_out.at[dy], twin_in.at[dy], gt_s.at[dy], gt_r.at[dy], {"vocab": twin}).wait_recv()
            both = total[i * band:(i + 1) * band] + twin_in[dy].astype(f32)
            rsend[g] = both.astype(bf16).reshape(nx, tb, feats)
            for dx in near(nx)[::-1]:
                if dy or dx:
                    oy, ox = other(dy, dx)
                    at = oy * nx + ox
                    copy = to(rsend.at[oy, ox], rrecv.at[chip], rs_s.at[at], rs_r.at[chip], {"vocab": at * 2 + core})
                    copy.start()
                    scatter.append(copy)

    block = dl[...].reshape(2 * ny * band, terms)
    gw[...] = jnp.dot(rows_t[...], block, preferred_element_type=f32).astype(bf16)

    rrecv[chip] = rsend[y, x]
    for dy, dx in offsets[1:]:
        oy, ox = other(dy, dx)
        at = oy * nx + ox
        to(rsend.at[oy, ox], rrecv.at[at], rs_s.at[at], rs_r.at[at], {"vocab": twin}).wait_recv()
    total = rrecv[0].astype(f32)
    for k in range(1, chips):
        total = total + rrecv[k].astype(f32)
    gh[...] = total.astype(bf16)
    for copy in gather + forward + ask + answer + halves + scatter:
        copy.wait_send()


def per_device(nx, nz, hidden, head_weight, grad_pooled, lengths, argmax_local):
    tb, feats = hidden.shape
    terms = head_weight.shape[1]
    passages = lengths.shape[0]
    chips = lax.axis_size("vocab") // 2
    ny = chips // nx
    band = nx * tb
    tokens = 2 * ny * band
    share = terms // nz
    anywhere = pl.BlockSpec(memory_space=pl.ANY)
    dma = pltpu.SemaphoreType.DMA
    return pl.pallas_call(
        functools.partial(kernel, ny, nx, nz),
        out_shape=(pltpu.VMEM((tb, feats), bf16), pltpu.VMEM((feats, terms), bf16)),
        in_specs=[pl.BlockSpec(memory_space=pltpu.SMEM)] + [anywhere] * 4,
        out_specs=(pl.BlockSpec(memory_space=pltpu.VMEM), pl.BlockSpec(memory_space=pltpu.VMEM)),
        scratch_shapes=[
            pltpu.VMEM((2, ny, nx, tb, feats), bf16),
            pltpu.VMEM((feats, tokens), bf16),
            pltpu.VMEM((feats, terms), bf16),
            pltpu.VMEM((terms, feats), bf16),
            pltpu.VMEM((2, ny, band, terms), bf16),
            pltpu.VMEM((2, ny, band, terms), bf16),
            pltpu.VMEM((passages, terms), jnp.int32),
            pltpu.VMEM((passages, share), f32),
            pltpu.VMEM((2, ny, band, passages), bf16),
            pltpu.VMEM((2, ny, passages, band), bf16),
            pltpu.VMEM((nz, passages, share), f32),
            pltpu.VMEM((nz, passages, share), bf16),
            pltpu.VMEM((nz, passages, share), bf16),
            pltpu.VMEM((nz, passages, share), bf16),
            pltpu.VMEM((ny, band, feats), bf16),
            pltpu.VMEM((ny, band, feats), bf16),
            pltpu.VMEM((ny, nx, tb, feats), bf16),
            pltpu.VMEM((chips, tb, feats), bf16),
            dma((4,)),
            dma((chips,)), dma((chips,)),
            dma((ny,)), dma((ny,)),
            dma((nz,)), dma((nz,)),
            dma((nz,)), dma((nz,)),
            dma((ny,)), dma((ny,)),
            dma((chips,)), dma((chips,)),
        ],
        compiler_params=pltpu.CompilerParams(
            collective_id=0, has_side_effects=True, vmem_limit_bytes=56 * 1024 * 1024
        ),
        cost_estimate=pl.CostEstimate(
            flops=6 * tokens * feats * terms, bytes_accessed=4 * feats * terms, transcendentals=0
        ),
    )(lengths, hidden, head_weight, grad_pooled, argmax_local)


def solution(mesh):
    in_specs = (P("vocab", "dp"), P("dp", "vocab"), P(None, "vocab"), P(), P(None, "vocab"))
    out_specs = (P("vocab", "dp"), P("dp", "vocab"))
    nx = 4 if mesh.shape["vocab"] == 32 else 2
    return jax.shard_map(
        functools.partial(per_device, nx, mesh.shape["dp"]),
        mesh=mesh, in_specs=in_specs, out_specs=out_specs, check_vma=False,
    )
```

```python
import functools

import jax
import jax.numpy as jnp
from jax import lax
from jax.experimental import pallas as pl
from jax.experimental.pallas import tpu as pltpu
from jax.sharding import PartitionSpec as P

flops_weight = 3.0
MESH = pl.DeviceIdType.MESH
f32, bf16 = jnp.float32, jnp.bfloat16
CUT = 4
PIECES = 2


def kernel(
    ny, nx, nz,
    len_hbm, hid, w_hbm, gp_hbm, am_hbm,
    gh, gw,
    rows, rows_t, w, w_t, mask, dl, am, gp, e, e_t, part, give, take, slopes,
    twin_out, twin_in, rsend, rrecv, len_ref,
    loc_sem, ag_s, ag_r, tw_s, tw_r, x1_s, x1_r, x2_s, x2_r, gt_s, gt_r, rs_s, rs_r,
):
    chips = ny * nx
    me, z = lax.axis_index("vocab"), lax.axis_index("dp")
    core, chip = lax.rem(me, 2), lax.div(me, 2)
    x, y = lax.rem(chip, nx), lax.div(chip, nx)
    mate = 1 - core
    twin = chip * 2 + mate
    tb, feats = hid.shape
    terms = w.shape[1]
    passages = len_hbm.shape[0]
    band = nx * tb
    share = terms // nz
    wide = terms // CUT

    def to(src, dst, s, r, device):
        return pltpu.make_async_remote_copy(
            src_ref=src, dst_ref=dst, send_sem=s, recv_sem=r, device_id=device, device_id_type=MESH
        )

    near = lambda n: sorted(range(n), key=lambda d: (min(d, n - d), d))
    offsets = [(dy, dx) for dy in near(ny) for dx in near(nx)]
    far_xy = sorted(offsets[1:], key=lambda o: -min(o[0], ny - o[0]) - min(o[1], nx - o[1]))
    far_z = near(nz)[:0:-1]
    other = lambda dy, dx: (lax.rem(y + dy, ny), lax.rem(x + dx, nx))

    barrier = pltpu.get_barrier_semaphore()
    for dy, dx in far_xy:
        oy, ox = other(dy, dx)
        pl.semaphore_signal(barrier, inc=1, device_id={"vocab": (oy * nx + ox) * 2 + core}, device_id_type=MESH)
    pl.semaphore_signal(barrier, inc=1, device_id={"vocab": twin}, device_id_type=MESH)
    for k in far_z:
        pl.semaphore_signal(barrier, inc=1, device_id={"dp": lax.rem(z + k, nz)}, device_id_type=MESH)

    local = [
        pltpu.make_async_copy(hid, rows.at[core, y, x], loc_sem.at[0]),
        pltpu.make_async_copy(len_hbm, len_ref, loc_sem.at[4]),
        pltpu.make_async_copy(am_hbm, am, loc_sem.at[1]),
        pltpu.make_async_copy(w_hbm, w, loc_sem.at[2]),
        pltpu.make_async_copy(gp_hbm.at[:, pl.ds(pl.multiple_of(z * share, share), share)], gp, loc_sem.at[3]),
    ]
    for copy in local:
        copy.start()

    local[0].wait()
    pl.semaphore_wait(barrier, chips + nz - 1)

    gather = []
    for dy, dx in far_xy:
        oy, ox = other(dy, dx)
        at = oy * nx + ox
        copy = to(rows.at[core, y, x], rows.at[core, y, x], ag_s.at[at], ag_r.at[chip], {"vocab": at * 2 + core})
        copy.start()
        gather.append(copy)

    local[1].wait()
    starts, begin = [], jnp.int32(0)
    for p in range(passages):
        starts.append(begin)
        begin = begin + len_ref[p]
    ends = starts[1:] + [begin]

    def tokens(shape, dim, c, g):
        i = lax.broadcasted_iota(jnp.int32, shape, dim)
        return i + jnp.bitwise_and(i, -tb) + (g * 2 * band + c * tb)

    lane = lax.broadcasted_iota(jnp.int32, (band, passages), 1)
    first = jnp.zeros((band, passages), jnp.int32)
    last = jnp.zeros((band, passages), jnp.int32)
    sub = lax.broadcasted_iota(jnp.int32, (passages, band), 0)
    first_t = jnp.zeros((passages, band), jnp.int32)
    last_t = jnp.zeros((passages, band), jnp.int32)
    for p in range(passages):
        first = jnp.where(lane == p, starts[p], first)
        last = jnp.where(lane == p, ends[p], last)
        first_t = jnp.where(sub == p, starts[p], first_t)
        last_t = jnp.where(sub == p, ends[p], last_t)
    for c in range(2):
        for g in range(ny):
            token = tokens((band, passages), 0, c, g)
            e[c, g] = jnp.where((token >= first) & (token < last), 1.0, 0.0).astype(bf16)
            token = tokens((passages, band), 1, c, g)
            e_t[c, g] = jnp.where((token >= first_t) & (token < last_t), 1.0, 0.0).astype(bf16)
    local[2].wait()

    def mark(c, carry):
        places = []
        for g in range(ny):
            token = tokens((band, 1), 0, c, g)
            place = token
            for p in range(1, passages):
                place = jnp.where(token >= starts[p], token - starts[p], place)
            places.append(place)
        place = jnp.concatenate(places, axis=0).astype(f32)
        member = e[c].reshape(ny * band, passages)
        for n in range(CUT):
            cols = slice(n * wide, (n + 1) * wide)
            spread = jnp.dot(member, am[:, cols].astype(f32).astype(bf16), preferred_element_type=f32)
            mask[c, :, :, cols] = jnp.where(spread == place, 1.0, 0.0).astype(bf16).reshape(ny, band, wide)
        return carry

    lax.fori_loop(0, 2, mark, 0)
    local[3].wait()
    for n in range(CUT):
        w_t[n * wide:(n + 1) * wide, :] = w[:, n * wide:(n + 1) * wide].T

    def pick(c, bands, start):
        block = jnp.concatenate([rows[c, g].reshape(band, feats) for g in bands], axis=0)
        member = jnp.concatenate([e_t[c, g] for g in bands], axis=1)
        logits = jnp.dot(block, w[...], preferred_element_type=f32)
        marks = jnp.concatenate([mask[c, g] for g in bands], axis=0)
        found = jnp.dot(member, logits.astype(bf16) * marks, preferred_element_type=f32)
        for j in range(nz):
            piece = found[:, j * share:(j + 1) * share]
            part[j] = piece if start else part[j] + piece

    near_y = near(ny)
    pairs = [near_y[::-1][:ny // 2], near_y[::-1][ny // 2:]]
    parts = [near_y[::-1][:ny // 2], near_y[::-1][ny // 2:]]
    forward = []
    for s, pair in enumerate(pairs):
        bands = [lax.rem(y + dy, ny) for dy in pair]
        for dy, g in zip(pair, bands):
            for dx in near(nx):
                if dy or dx:
                    oy, ox = other(dy, dx)
                    at = oy * nx + ox
                    to(rows.at[core, oy, ox], rows.at[core, oy, ox], ag_s.at[at], ag_r.at[at], {"vocab": twin}).wait_recv()
            copy = to(rows.at[core, g], rows.at[core, g], tw_s.at[dy], tw_r.at[dy], {"vocab": twin})
            copy.start()
            forward.append(copy)
        pick(core, bands, s == 0)
        for dy, g in zip(pair, bands):
            to(rows.at[mate, g], rows.at[mate, g], tw_s.at[dy], tw_r.at[dy], {"vocab": twin}).wait_recv()
        pick(mate, bands, False)

    for j in range(nz):
        give[j] = part[j].astype(bf16)
    ask = []
    for k in far_z:
        oz = lax.rem(z + k, nz)
        copy = to(give.at[oz], take.at[z], x1_s.at[oz], x1_r.at[z], {"dp": oz})
        copy.start()
        ask.append(copy)
    take[z] = give[z]
    for c in range(2):
        rows_t[:, c * ny * band:(c + 1) * ny * band] = rows[c].reshape(ny * band, feats).T
    for k in far_z:
        oz = lax.rem(z + k, nz)
        to(give.at[oz], take.at[oz], x1_s.at[oz], x1_r.at[oz], {"dp": oz}).wait_recv()
    local[4].wait()
    picked = take[0].astype(f32)
    for j in range(1, nz):
        picked = picked + take[j].astype(f32)
    small = jnp.exp(-jnp.abs(picked))
    soft = jnp.maximum(picked, 0.0) + jnp.log1p(small)
    column = jnp.sum(jnp.log1p(soft), axis=0, keepdims=True)
    upstream = gp[...] + 2.0 * flops_weight / (passages * passages) * column
    sigmoid = jnp.where(picked >= 0, 1.0, small) / (1.0 + small)
    slopes[z] = (upstream * sigmoid / (1.0 + soft)).astype(bf16)
    answer = []
    for k in far_z:
        oz = lax.rem(z + k, nz)
        copy = to(slopes.at[z], slopes.at[z], x2_s.at[oz], x2_r.at[z], {"dp": oz})
        copy.start()
        answer.append(copy)
    for k in far_z:
        oz = lax.rem(z + k, nz)
        to(slopes.at[z], slopes.at[oz], x2_s.at[oz], x2_r.at[oz], {"dp": oz}).wait_recv()

    def spread_slopes(c, bands):
        member = jnp.concatenate([e[c, g] for g in bands], axis=0)
        slope = jnp.concatenate([slopes[j] for j in range(nz)], axis=1)
        wider = jnp.dot(member, slope, preferred_element_type=f32).astype(bf16)
        for i, g in enumerate(bands):
            dl[c, g] = wider[i * band:(i + 1) * band] * mask[c, g]

    def hidden_part(c, bands):
        block = jnp.concatenate([dl[c, g] for g in bands], axis=0)
        return jnp.dot(block, w_t[...], preferred_element_type=f32)

    scatter, halves = [], []
    for pair in parts:
        bands = [lax.rem(y + dy, ny) for dy in pair]
        spread_slopes(mate, bands)
        total = hidden_part(mate, bands).astype(bf16)
        for i, dy in enumerate(pair):
            twin_out[dy] = total[i * band:(i + 1) * band]
            copy = to(twin_out.at[dy], twin_in.at[dy], gt_s.at[dy], gt_r.at[dy], {"vocab": twin})
            copy.start()
            halves.append(copy)
    for pair in parts:
        bands = [lax.rem(y + dy, ny) for dy in pair]
        spread_slopes(core, bands)
        total = hidden_part(core, bands)
        for i, (dy, g) in enumerate(zip(pair, bands)):
            to(twin_out.at[dy], twin_in.at[dy], gt_s.at[dy], gt_r.at[dy], {"vocab": twin}).wait_recv()
            both = total[i * band:(i + 1) * band] + twin_in[dy].astype(f32)
            rsend[g] = both.astype(bf16).reshape(nx, tb, feats)
            for dx in near(nx)[::-1]:
                if dy or dx:
                    oy, ox = other(dy, dx)
                    at = oy * nx + ox
                    copy = to(rsend.at[oy, ox], rrecv.at[chip], rs_s.at[at], rs_r.at[chip], {"vocab": at * 2 + core})
                    copy.start()
                    scatter.append(copy)

    block = dl[...].reshape(2 * ny * band, terms)
    gw[...] = jnp.dot(rows_t[...], block, preferred_element_type=f32).astype(bf16)

    rrecv[chip] = rsend[y, x]
    for copy in gather + forward + ask + answer + halves:
        copy.wait_send()
    for dy, dx in offsets[1:]:
        oy, ox = other(dy, dx)
        at = oy * nx + ox
        to(rsend.at[oy, ox], rrecv.at[at], rs_s.at[at], rs_r.at[at], {"vocab": twin}).wait_recv()
    total = rrecv[0].astype(f32)
    for k in range(1, chips):
        total = total + rrecv[k].astype(f32)
    gh[...] = total.astype(bf16)
    for copy in scatter:
        copy.wait_send()


def finish(gh, gw, gh_out, gw_out, sem):
    high = gw.shape[0] // PIECES
    copies = [
        pltpu.make_async_copy(gw.at[pl.ds(n * high, high)], gw_out.at[pl.ds(n * high, high)], sem.at[n])
        for n in range(PIECES)
    ]
    copies.append(pltpu.make_async_copy(gh, gh_out, sem.at[PIECES]))
    for copy in copies:
        copy.start()
    for copy in copies:
        copy.wait()


def per_device(nx, nz, hidden, head_weight, grad_pooled, lengths, argmax_local):
    tb, feats = hidden.shape
    terms = head_weight.shape[1]
    passages = lengths.shape[0]
    chips = lax.axis_size("vocab") // 2
    ny = chips // nx
    band = nx * tb
    tokens = 2 * ny * band
    share = terms // nz
    anywhere = pl.BlockSpec(memory_space=pl.ANY)
    dma = pltpu.SemaphoreType.DMA
    gh, gw = pl.pallas_call(
        functools.partial(kernel, ny, nx, nz),
        out_shape=(pltpu.VMEM((tb, feats), bf16), pltpu.VMEM((feats, terms), bf16)),
        in_specs=[anywhere] * 5,
        out_specs=(pl.BlockSpec(memory_space=pltpu.VMEM), pl.BlockSpec(memory_space=pltpu.VMEM)),
        scratch_shapes=[
            pltpu.VMEM((2, ny, nx, tb, feats), bf16),
            pltpu.VMEM((feats, tokens), bf16),
            pltpu.VMEM((feats, terms), bf16),
            pltpu.VMEM((terms, feats), bf16),
            pltpu.VMEM((2, ny, band, terms), bf16),
            pltpu.VMEM((2, ny, band, terms), bf16),
            pltpu.VMEM((passages, terms), jnp.int32),
            pltpu.VMEM((passages, share), f32),
            pltpu.VMEM((2, ny, band, passages), bf16),
            pltpu.VMEM((2, ny, passages, band), bf16),
            pltpu.VMEM((nz, passages, share), f32),
            pltpu.VMEM((nz, passages, share), bf16),
            pltpu.VMEM((nz, passages, share), bf16),
            pltpu.VMEM((nz, passages, share), bf16),
            pltpu.VMEM((ny, band, feats), bf16),
            pltpu.VMEM((ny, band, feats), bf16),
            pltpu.VMEM((ny, nx, tb, feats), bf16),
            pltpu.VMEM((chips, tb, feats), bf16),
            pltpu.SMEM((passages,), jnp.int32),
            dma((5,)),
            dma((chips,)), dma((chips,)),
            dma((ny,)), dma((ny,)),
            dma((nz,)), dma((nz,)),
            dma((nz,)), dma((nz,)),
            dma((ny,)), dma((ny,)),
            dma((chips,)), dma((chips,)),
        ],
        compiler_params=pltpu.CompilerParams(
            collective_id=0, has_side_effects=True, vmem_limit_bytes=56 * 1024 * 1024
        ),
        cost_estimate=pl.CostEstimate(
            flops=6 * tokens * feats * terms, bytes_accessed=4 * feats * terms, transcendentals=0
        ),
    )(lengths, hidden, head_weight, grad_pooled, argmax_local)
    return pl.pallas_call(
        finish,
        out_shape=(
            jax.ShapeDtypeStruct((tb, feats), bf16),
            jax.ShapeDtypeStruct((feats, terms), bf16),
        ),
        in_specs=[anywhere] * 2,
        out_specs=(anywhere, anywhere),
        scratch_shapes=[dma((PIECES + 1,))],
        compiler_params=pltpu.CompilerParams(vmem_limit_bytes=1024 * 1024),
    )(gh, gw)


def solution(mesh):
    in_specs = (P("vocab", "dp"), P("dp", "vocab"), P(None, "vocab"), P(), P(None, "vocab"))
    out_specs = (P("vocab", "dp"), P("dp", "vocab"))
    nx = 4 if mesh.shape["vocab"] == 32 else 2
    return jax.shard_map(
        functools.partial(per_device, nx, mesh.shape["dp"]),
        mesh=mesh, in_specs=in_specs, out_specs=out_specs, check_vma=False,
    )
```

```python
import functools

import jax
import jax.numpy as jnp
from jax import lax
from jax.experimental import pallas as pl
from jax.experimental.pallas import tpu as pltpu
from jax.sharding import PartitionSpec as P

flops_weight = 3.0
MESH = pl.DeviceIdType.MESH
f32, bf16 = jnp.float32, jnp.bfloat16
CUT = 4
PIECES = 2


def kernel(
    ny, nx, nz,
    len_hbm, hid, w_hbm, gp_hbm, am_hbm,
    gh, gw,
    rows, rows_t, w, w_t, mask, dl, am, gp, e, e_t, part, give, take, slopes,
    twin_out, twin_in, rsend, rrecv, len_ref,
    loc_sem, ag_s, ag_r, tw_s, tw_r, x1_s, x1_r, x2_s, x2_r, gt_s, gt_r, rs_s, rs_r,
):
    chips = ny * nx
    me, z = lax.axis_index("vocab"), lax.axis_index("dp")
    core, chip = lax.rem(me, 2), lax.div(me, 2)
    x, y = lax.rem(chip, nx), lax.div(chip, nx)
    mate = 1 - core
    twin = chip * 2 + mate
    tb, feats = hid.shape
    terms = w.shape[1]
    passages = len_hbm.shape[0]
    band = nx * tb
    share = terms // nz
    wide = terms // CUT

    def to(src, dst, s, r, device):
        return pltpu.make_async_remote_copy(
            src_ref=src, dst_ref=dst, send_sem=s, recv_sem=r, device_id=device, device_id_type=MESH
        )

    near = lambda n: sorted(range(n), key=lambda d: (min(d, n - d), d))
    offsets = [(dy, dx) for dy in near(ny) for dx in near(nx)]
    far_xy = sorted(offsets[1:], key=lambda o: -min(o[0], ny - o[0]) - min(o[1], nx - o[1]))
    far_z = near(nz)[:0:-1]
    other = lambda dy, dx: (lax.rem(y + dy, ny), lax.rem(x + dx, nx))

    barrier = pltpu.get_barrier_semaphore()
    for dy, dx in far_xy:
        oy, ox = other(dy, dx)
        pl.semaphore_signal(barrier, inc=1, device_id={"vocab": (oy * nx + ox) * 2 + core}, device_id_type=MESH)
    pl.semaphore_signal(barrier, inc=1, device_id={"vocab": twin}, device_id_type=MESH)
    for k in far_z:
        pl.semaphore_signal(barrier, inc=1, device_id={"dp": lax.rem(z + k, nz)}, device_id_type=MESH)

    local = [
        pltpu.make_async_copy(hid, rows.at[core, y, x], loc_sem.at[0]),
        pltpu.make_async_copy(len_hbm, len_ref, loc_sem.at[4]),
        pltpu.make_async_copy(am_hbm, am, loc_sem.at[1]),
        pltpu.make_async_copy(w_hbm, w, loc_sem.at[2]),
        pltpu.make_async_copy(gp_hbm.at[:, pl.ds(pl.multiple_of(z * share, share), share)], gp, loc_sem.at[3]),
    ]
    for copy in local:
        copy.start()

    local[0].wait()
    pl.semaphore_wait(barrier, chips + nz - 1)

    gather = []
    for dy, dx in far_xy:
        oy, ox = other(dy, dx)
        at = oy * nx + ox
        copy = to(rows.at[core, y, x], rows.at[core, y, x], ag_s.at[at], ag_r.at[chip], {"vocab": at * 2 + core})
        copy.start()
        gather.append(copy)

    local[1].wait()
    starts, begin = [], jnp.int32(0)
    for p in range(passages):
        starts.append(begin)
        begin = begin + len_ref[p]
    ends = starts[1:] + [begin]

    def tokens(shape, dim, c, g):
        i = lax.broadcasted_iota(jnp.int32, shape, dim)
        return i + jnp.bitwise_and(i, -tb) + (g * 2 * band + c * tb)

    lane = lax.broadcasted_iota(jnp.int32, (band, passages), 1)
    first = jnp.zeros((band, passages), jnp.int32)
    last = jnp.zeros((band, passages), jnp.int32)
    sub = lax.broadcasted_iota(jnp.int32, (passages, band), 0)
    first_t = jnp.zeros((passages, band), jnp.int32)
    last_t = jnp.zeros((passages, band), jnp.int32)
    for p in range(passages):
        first = jnp.where(lane == p, starts[p], first)
        last = jnp.where(lane == p, ends[p], last)
        first_t = jnp.where(sub == p, starts[p], first_t)
        last_t = jnp.where(sub == p, ends[p], last_t)
    for c in range(2):
        for g in range(ny):
            token = tokens((band, passages), 0, c, g)
            e[c, g] = jnp.where((token >= first) & (token < last), 1.0, 0.0).astype(bf16)
            token = tokens((passages, band), 1, c, g)
            e_t[c, g] = jnp.where((token >= first_t) & (token < last_t), 1.0, 0.0).astype(bf16)
    local[2].wait()

    def mark(c, carry):
        places = []
        for g in range(ny):
            token = tokens((band, 1), 0, c, g)
            place = token
            for p in range(1, passages):
                place = jnp.where(token >= starts[p], token - starts[p], place)
            places.append(place)
        place = jnp.concatenate(places, axis=0).astype(f32)
        member = e[c].reshape(ny * band, passages)
        for n in range(CUT):
            cols = slice(n * wide, (n + 1) * wide)
            spread = jnp.dot(member, am[:, cols].astype(f32).astype(bf16), preferred_element_type=f32)
            mask[c, :, :, cols] = jnp.where(spread == place, 1.0, 0.0).astype(bf16).reshape(ny, band, wide)
        return carry

    lax.fori_loop(0, 2, mark, 0)
    local[3].wait()
    for n in range(CUT):
        w_t[n * wide:(n + 1) * wide, :] = w[:, n * wide:(n + 1) * wide].T

    def pick(c, bands, start):
        block = jnp.concatenate([rows[c, g].reshape(band, feats) for g in bands], axis=0)
        member = jnp.concatenate([e_t[c, g] for g in bands], axis=1)
        logits = jnp.dot(block, w[...], preferred_element_type=f32)
        marks = jnp.concatenate([mask[c, g] for g in bands], axis=0)
        found = jnp.dot(member, logits.astype(bf16) * marks, preferred_element_type=f32)
        for j in range(nz):
            piece = found[:, j * share:(j + 1) * share]
            part[j] = piece if start else part[j] + piece

    near_y = near(ny)
    pairs = [near_y[::-1][:ny // 2], near_y[::-1][ny // 2:]]
    far_y = near_y[::-1]
    parts = [far_y[::2], far_y[1::2]]
    forward = []

    def bands_of(pair):
        return [lax.rem(y + dy, ny) for dy in pair]

    def arrive(pair):
        for dy, g in zip(pair, bands_of(pair)):
            for dx in near(nx):
                if dy or dx:
                    oy, ox = other(dy, dx)
                    at = oy * nx + ox
                    to(rows.at[core, oy, ox], rows.at[core, oy, ox], ag_s.at[at], ag_r.at[at], {"vocab": twin}).wait_recv()
            copy = to(rows.at[core, g], rows.at[core, g], tw_s.at[dy], tw_r.at[dy], {"vocab": twin})
            copy.start()
            forward.append(copy)

    def lent(pair):
        for dy, g in zip(pair, bands_of(pair)):
            to(rows.at[mate, g], rows.at[mate, g], tw_s.at[dy], tw_r.at[dy], {"vocab": twin}).wait_recv()

    first_pair, second_pair = pairs
    arrive(first_pair)
    pick(core, bands_of(first_pair), True)
    arrive(second_pair)
    lent(first_pair)
    pick(mate, bands_of(first_pair), False)
    pick(core, bands_of(second_pair), False)
    lent(second_pair)
    pick(mate, bands_of(second_pair), False)

    for j in range(nz):
        give[j] = part[j].astype(bf16)
    ask = []
    for k in far_z:
        oz = lax.rem(z + k, nz)
        copy = to(give.at[oz], take.at[z], x1_s.at[oz], x1_r.at[z], {"dp": oz})
        copy.start()
        ask.append(copy)
    take[z] = give[z]
    for k in far_z:
        oz = lax.rem(z + k, nz)
        to(give.at[oz], take.at[oz], x1_s.at[oz], x1_r.at[oz], {"dp": oz}).wait_recv()
    local[4].wait()
    picked = take[0].astype(f32)
    for j in range(1, nz):
        picked = picked + take[j].astype(f32)
    small = jnp.exp(-jnp.abs(picked))
    soft = jnp.maximum(picked, 0.0) + jnp.log1p(small)
    column = jnp.sum(jnp.log1p(soft), axis=0, keepdims=True)
    upstream = gp[...] + 2.0 * flops_weight / (passages * passages) * column
    sigmoid = jnp.where(picked >= 0, 1.0, small) / (1.0 + small)
    slopes[z] = (upstream * sigmoid / (1.0 + soft)).astype(bf16)
    answer = []
    for k in far_z:
        oz = lax.rem(z + k, nz)
        copy = to(slopes.at[z], slopes.at[z], x2_s.at[oz], x2_r.at[z], {"dp": oz})
        copy.start()
        answer.append(copy)
    for k in far_z:
        oz = lax.rem(z + k, nz)
        to(slopes.at[z], slopes.at[oz], x2_s.at[oz], x2_r.at[oz], {"dp": oz}).wait_recv()

    def spread_slopes(c, bands):
        member = jnp.concatenate([e[c, g] for g in bands], axis=0)
        slope = jnp.concatenate([slopes[j] for j in range(nz)], axis=1)
        wider = jnp.dot(member, slope, preferred_element_type=f32).astype(bf16)
        for i, g in enumerate(bands):
            dl[c, g] = wider[i * band:(i + 1) * band] * mask[c, g]

    def hidden_part(c, bands):
        block = jnp.concatenate([dl[c, g] for g in bands], axis=0)
        return jnp.dot(block, w_t[...], preferred_element_type=f32)

    scatter, halves = [], []
    for pair in parts:
        bands = [lax.rem(y + dy, ny) for dy in pair]
        spread_slopes(mate, bands)
        total = hidden_part(mate, bands).astype(bf16)
        for i, dy in enumerate(pair):
            twin_out[dy] = total[i * band:(i + 1) * band]
            copy = to(twin_out.at[dy], twin_in.at[dy], gt_s.at[dy], gt_r.at[dy], {"vocab": twin})
            copy.start()
            halves.append(copy)
    for pair in parts:
        bands = [lax.rem(y + dy, ny) for dy in pair]
        spread_slopes(core, bands)
        total = hidden_part(core, bands)
        for i, (dy, g) in enumerate(zip(pair, bands)):
            to(twin_out.at[dy], twin_in.at[dy], gt_s.at[dy], gt_r.at[dy], {"vocab": twin}).wait_recv()
            both = total[i * band:(i + 1) * band] + twin_in[dy].astype(f32)
            rsend[g] = both.astype(bf16).reshape(nx, tb, feats)
            for dx in near(nx)[::-1]:
                if dy or dx:
                    oy, ox = other(dy, dx)
                    at = oy * nx + ox
                    copy = to(rsend.at[oy, ox], rrecv.at[chip], rs_s.at[at], rs_r.at[chip], {"vocab": at * 2 + core})
                    copy.start()
                    scatter.append(copy)

    for c in range(2):
        rows_t[:, c * ny * band:(c + 1) * ny * band] = rows[c].reshape(ny * band, feats).T
    block = dl[...].reshape(2 * ny * band, terms)
    gw[...] = jnp.dot(rows_t[...], block, preferred_element_type=f32).astype(bf16)

    rrecv[chip] = rsend[y, x]
    for copy in gather + forward + ask + answer + halves:
        copy.wait_send()
    for dy, dx in offsets[1:]:
        oy, ox = other(dy, dx)
        at = oy * nx + ox
        to(rsend.at[oy, ox], rrecv.at[at], rs_s.at[at], rs_r.at[at], {"vocab": twin}).wait_recv()
    total = rrecv[0].astype(f32)
    for k in range(1, chips):
        total = total + rrecv[k].astype(f32)
    gh[...] = total.astype(bf16)
    for copy in scatter:
        copy.wait_send()


def finish(gh, gw, gh_out, gw_out, sem):
    high = gw.shape[0] // PIECES
    copies = [
        pltpu.make_async_copy(gw.at[pl.ds(n * high, high)], gw_out.at[pl.ds(n * high, high)], sem.at[n])
        for n in range(PIECES)
    ]
    copies.append(pltpu.make_async_copy(gh, gh_out, sem.at[PIECES]))
    for copy in copies:
        copy.start()
    for copy in copies:
        copy.wait()


def per_device(nx, nz, hidden, head_weight, grad_pooled, lengths, argmax_local):
    tb, feats = hidden.shape
    terms = head_weight.shape[1]
    passages = lengths.shape[0]
    chips = lax.axis_size("vocab") // 2
    ny = chips // nx
    band = nx * tb
    tokens = 2 * ny * band
    share = terms // nz
    anywhere = pl.BlockSpec(memory_space=pl.ANY)
    dma = pltpu.SemaphoreType.DMA
    gh, gw = pl.pallas_call(
        functools.partial(kernel, ny, nx, nz),
        out_shape=(pltpu.VMEM((tb, feats), bf16), pltpu.VMEM((feats, terms), bf16)),
        in_specs=[anywhere] * 5,
        out_specs=(pl.BlockSpec(memory_space=pltpu.VMEM), pl.BlockSpec(memory_space=pltpu.VMEM)),
        scratch_shapes=[
            pltpu.VMEM((2, ny, nx, tb, feats), bf16),
            pltpu.VMEM((feats, tokens), bf16),
            pltpu.VMEM((feats, terms), bf16),
            pltpu.VMEM((terms, feats), bf16),
            pltpu.VMEM((2, ny, band, terms), bf16),
            pltpu.VMEM((2, ny, band, terms), bf16),
            pltpu.VMEM((passages, terms), jnp.int32),
            pltpu.VMEM((passages, share), f32),
            pltpu.VMEM((2, ny, band, passages), bf16),
            pltpu.VMEM((2, ny, passages, band), bf16),
            pltpu.VMEM((nz, passages, share), f32),
            pltpu.VMEM((nz, passages, share), bf16),
            pltpu.VMEM((nz, passages, share), bf16),
            pltpu.VMEM((nz, passages, share), bf16),
            pltpu.VMEM((ny, band, feats), bf16),
            pltpu.VMEM((ny, band, feats), bf16),
            pltpu.VMEM((ny, nx, tb, feats), bf16),
            pltpu.VMEM((chips, tb, feats), bf16),
            pltpu.SMEM((passages,), jnp.int32),
            dma((5,)),
            dma((chips,)), dma((chips,)),
            dma((ny,)), dma((ny,)),
            dma((nz,)), dma((nz,)),
            dma((nz,)), dma((nz,)),
            dma((ny,)), dma((ny,)),
            dma((chips,)), dma((chips,)),
        ],
        compiler_params=pltpu.CompilerParams(
            collective_id=0, has_side_effects=True, vmem_limit_bytes=56 * 1024 * 1024
        ),
        cost_estimate=pl.CostEstimate(
            flops=6 * tokens * feats * terms, bytes_accessed=4 * feats * terms, transcendentals=0
        ),
    )(lengths, hidden, head_weight, grad_pooled, argmax_local)
    return pl.pallas_call(
        finish,
        out_shape=(
            jax.ShapeDtypeStruct((tb, feats), bf16),
            jax.ShapeDtypeStruct((feats, terms), bf16),
        ),
        in_specs=[anywhere] * 2,
        out_specs=(anywhere, anywhere),
        scratch_shapes=[dma((PIECES + 1,))],
        compiler_params=pltpu.CompilerParams(vmem_limit_bytes=1024 * 1024),
    )(gh, gw)


def solution(mesh):
    in_specs = (P("vocab", "dp"), P("dp", "vocab"), P(None, "vocab"), P(), P(None, "vocab"))
    out_specs = (P("vocab", "dp"), P("dp", "vocab"))
    nx = 4 if mesh.shape["vocab"] == 32 else 2
    return jax.shard_map(
        functools.partial(per_device, nx, mesh.shape["dp"]),
        mesh=mesh, in_specs=in_specs, out_specs=out_specs, check_vma=False,
    )
```

```python
import functools

import jax
import jax.numpy as jnp
from jax import lax
from jax.experimental import pallas as pl
from jax.experimental.pallas import tpu as pltpu
from jax.sharding import PartitionSpec as P

flops_weight = 3.0
MESH = pl.DeviceIdType.MESH
f32, bf16 = jnp.float32, jnp.bfloat16
CUT = 4
PIECES = 2


def kernel(
    ny, nx, nz,
    len_hbm, hid, w_hbm, gp_hbm, am_hbm,
    gh, gw,
    rows, rows_t, w, w_t, mask, dl, am, gp, e, e_t, part, give, take, slopes,
    twin_out, twin_in, rsend, rrecv, len_ref,
    loc_sem, ag_s, ag_r, tw_s, tw_r, x1_s, x1_r, x2_s, x2_r, gt_s, gt_r, rs_s, rs_r,
):
    chips = ny * nx
    me, z = lax.axis_index("vocab"), lax.axis_index("dp")
    core, chip = lax.rem(me, 2), lax.div(me, 2)
    x, y = lax.rem(chip, nx), lax.div(chip, nx)
    mate = 1 - core
    twin = chip * 2 + mate
    tb, feats = hid.shape
    terms = w.shape[1]
    passages = len_hbm.shape[0]
    band = nx * tb
    share = terms // nz
    wide = terms // CUT

    def to(src, dst, s, r, device):
        return pltpu.make_async_remote_copy(
            src_ref=src, dst_ref=dst, send_sem=s, recv_sem=r, device_id=device, device_id_type=MESH
        )

    near = lambda n: sorted(range(n), key=lambda d: (min(d, n - d), d))
    offsets = [(dy, dx) for dy in near(ny) for dx in near(nx)]
    far_xy = sorted(offsets[1:], key=lambda o: -min(o[0], ny - o[0]) - min(o[1], nx - o[1]))
    far_z = near(nz)[:0:-1]
    other = lambda dy, dx: (lax.rem(y + dy, ny), lax.rem(x + dx, nx))

    barrier = pltpu.get_barrier_semaphore()
    for k in far_z:
        pl.semaphore_signal(barrier, inc=1, device_id={"dp": lax.rem(z + k, nz)}, device_id_type=MESH)
    for dy, dx in far_xy:
        oy, ox = other(dy, dx)
        pl.semaphore_signal(barrier, inc=1, device_id={"vocab": (oy * nx + ox) * 2 + core}, device_id_type=MESH)
    pl.semaphore_signal(barrier, inc=1, device_id={"vocab": twin}, device_id_type=MESH)

    local = [
        pltpu.make_async_copy(hid, rows.at[core, y, x], loc_sem.at[0]),
        pltpu.make_async_copy(len_hbm, len_ref, loc_sem.at[4]),
        pltpu.make_async_copy(am_hbm, am, loc_sem.at[1]),
        pltpu.make_async_copy(w_hbm, w, loc_sem.at[2]),
        pltpu.make_async_copy(gp_hbm.at[:, pl.ds(pl.multiple_of(z * share, share), share)], gp, loc_sem.at[3]),
    ]
    for copy in local:
        copy.start()

    local[0].wait()
    pl.semaphore_wait(barrier, chips + nz - 1)

    gather = []
    for dy, dx in far_xy:
        oy, ox = other(dy, dx)
        at = oy * nx + ox
        copy = to(rows.at[core, y, x], rows.at[core, y, x], ag_s.at[at], ag_r.at[chip], {"vocab": at * 2 + core})
        copy.start()
        gather.append(copy)

    local[1].wait()
    starts, begin = [], jnp.int32(0)
    for p in range(passages):
        starts.append(begin)
        begin = begin + len_ref[p]
    ends = starts[1:] + [begin]

    def tokens(shape, dim, c, g):
        i = lax.broadcasted_iota(jnp.int32, shape, dim)
        return i + jnp.bitwise_and(i, -tb) + (g * 2 * band + c * tb)

    lane = lax.broadcasted_iota(jnp.int32, (band, passages), 1)
    first = jnp.zeros((band, passages), jnp.int32)
    last = jnp.zeros((band, passages), jnp.int32)
    sub = lax.broadcasted_iota(jnp.int32, (passages, band), 0)
    first_t = jnp.zeros((passages, band), jnp.int32)
    last_t = jnp.zeros((passages, band), jnp.int32)
    for p in range(passages):
        first = jnp.where(lane == p, starts[p], first)
        last = jnp.where(lane == p, ends[p], last)
        first_t = jnp.where(sub == p, starts[p], first_t)
        last_t = jnp.where(sub == p, ends[p], last_t)
    for c in range(2):
        for g in range(ny):
            token = tokens((band, passages), 0, c, g)
            e[c, g] = jnp.where((token >= first) & (token < last), 1.0, 0.0).astype(bf16)
            token = tokens((passages, band), 1, c, g)
            e_t[c, g] = jnp.where((token >= first_t) & (token < last_t), 1.0, 0.0).astype(bf16)
    local[2].wait()

    def mark(c, carry):
        places = []
        for g in range(ny):
            token = tokens((band, 1), 0, c, g)
            place = token
            for p in range(1, passages):
                place = jnp.where(token >= starts[p], token - starts[p], place)
            places.append(place)
        place = jnp.concatenate(places, axis=0).astype(f32)
        member = e[c].reshape(ny * band, passages)
        for n in range(CUT):
            cols = slice(n * wide, (n + 1) * wide)
            spread = jnp.dot(member, am[:, cols].astype(f32).astype(bf16), preferred_element_type=f32)
            mask[c, :, :, cols] = jnp.where(spread == place, 1.0, 0.0).astype(bf16).reshape(ny, band, wide)
        return carry

    lax.fori_loop(0, 2, mark, 0)
    local[3].wait()
    for n in range(CUT):
        w_t[n * wide:(n + 1) * wide, :] = w[:, n * wide:(n + 1) * wide].T

    def pick(c, bands, start):
        block = jnp.concatenate([rows[c, g].reshape(band, feats) for g in bands], axis=0)
        member = jnp.concatenate([e_t[c, g] for g in bands], axis=1)
        logits = jnp.dot(block, w[...], preferred_element_type=f32)
        marks = jnp.concatenate([mask[c, g] for g in bands], axis=0)
        found = jnp.dot(member, logits.astype(bf16) * marks, preferred_element_type=f32)
        for j in range(nz):
            piece = found[:, j * share:(j + 1) * share]
            part[j] = piece if start else part[j] + piece

    near_y = near(ny)
    pairs = [near_y[::-1][:ny // 2], near_y[::-1][ny // 2:]]
    far_y = near_y[::-1]
    parts = [far_y[::2], far_y[1::2]]
    forward = []

    def bands_of(pair):
        return [lax.rem(y + dy, ny) for dy in pair]

    def arrive(pair):
        for dy, g in zip(pair, bands_of(pair)):
            for dx in near(nx):
                if dy or dx:
                    oy, ox = other(dy, dx)
                    at = oy * nx + ox
                    to(rows.at[core, oy, ox], rows.at[core, oy, ox], ag_s.at[at], ag_r.at[at], {"vocab": twin}).wait_recv()
            copy = to(rows.at[core, g], rows.at[core, g], tw_s.at[dy], tw_r.at[dy], {"vocab": twin})
            copy.start()
            forward.append(copy)

    def lent(pair):
        for dy, g in zip(pair, bands_of(pair)):
            to(rows.at[mate, g], rows.at[mate, g], tw_s.at[dy], tw_r.at[dy], {"vocab": twin}).wait_recv()

    first_pair, second_pair = pairs
    arrive(first_pair)
    pick(core, bands_of(first_pair), True)
    arrive(second_pair)
    lent(first_pair)
    pick(mate, bands_of(first_pair), False)
    pick(core, bands_of(second_pair), False)
    lent(second_pair)
    pick(mate, bands_of(second_pair), False)

    for j in range(nz):
        give[j] = part[j].astype(bf16)
    ask = []
    for k in far_z:
        oz = lax.rem(z + k, nz)
        copy = to(give.at[oz], take.at[z], x1_s.at[oz], x1_r.at[z], {"dp": oz})
        copy.start()
        ask.append(copy)
    take[z] = give[z]
    for k in far_z:
        oz = lax.rem(z + k, nz)
        to(give.at[oz], take.at[oz], x1_s.at[oz], x1_r.at[oz], {"dp": oz}).wait_recv()
    local[4].wait()
    picked = take[0].astype(f32)
    for j in range(1, nz):
        picked = picked + take[j].astype(f32)
    small = jnp.exp(-jnp.abs(picked))
    soft = jnp.maximum(picked, 0.0) + jnp.log1p(small)
    column = jnp.sum(jnp.log1p(soft), axis=0, keepdims=True)
    upstream = gp[...] + 2.0 * flops_weight / (passages * passages) * column
    sigmoid = jnp.where(picked >= 0, 1.0, small) / (1.0 + small)
    slopes[z] = (upstream * sigmoid / (1.0 + soft)).astype(bf16)
    answer = []
    for k in far_z:
        oz = lax.rem(z + k, nz)
        copy = to(slopes.at[z], slopes.at[z], x2_s.at[oz], x2_r.at[z], {"dp": oz})
        copy.start()
        answer.append(copy)
    for k in far_z:
        oz = lax.rem(z + k, nz)
        to(slopes.at[z], slopes.at[oz], x2_s.at[oz], x2_r.at[oz], {"dp": oz}).wait_recv()

    def spread_slopes(c, bands):
        member = jnp.concatenate([e[c, g] for g in bands], axis=0)
        slope = jnp.concatenate([slopes[j] for j in range(nz)], axis=1)
        wider = jnp.dot(member, slope, preferred_element_type=f32).astype(bf16)
        for i, g in enumerate(bands):
            dl[c, g] = wider[i * band:(i + 1) * band] * mask[c, g]

    def hidden_part(c, bands):
        block = jnp.concatenate([dl[c, g] for g in bands], axis=0)
        return jnp.dot(block, w_t[...], preferred_element_type=f32)

    scatter, halves = [], []
    for pair in parts:
        bands = [lax.rem(y + dy, ny) for dy in pair]
        spread_slopes(mate, bands)
        total = hidden_part(mate, bands).astype(bf16)
        for i, dy in enumerate(pair):
            twin_out[dy] = total[i * band:(i + 1) * band]
            copy = to(twin_out.at[dy], twin_in.at[dy], gt_s.at[dy], gt_r.at[dy], {"vocab": twin})
            copy.start()
            halves.append(copy)
    for pair in parts:
        bands = [lax.rem(y + dy, ny) for dy in pair]
        spread_slopes(core, bands)
        total = hidden_part(core, bands)
        for i, (dy, g) in enumerate(zip(pair, bands)):
            to(twin_out.at[dy], twin_in.at[dy], gt_s.at[dy], gt_r.at[dy], {"vocab": twin}).wait_recv()
            both = total[i * band:(i + 1) * band] + twin_in[dy].astype(f32)
            rsend[g] = both.astype(bf16).reshape(nx, tb, feats)
            for dx in near(nx)[::-1]:
                if dy or dx:
                    oy, ox = other(dy, dx)
                    at = oy * nx + ox
                    copy = to(rsend.at[oy, ox], rrecv.at[chip], rs_s.at[at], rs_r.at[chip], {"vocab": at * 2 + core})
                    copy.start()
                    scatter.append(copy)

    for c in range(2):
        rows_t[:, c * ny * band:(c + 1) * ny * band] = rows[c].reshape(ny * band, feats).T
    block = dl[...].reshape(2 * ny * band, terms)
    gw[...] = jnp.dot(rows_t[...], block, preferred_element_type=f32).astype(bf16)

    rrecv[chip] = rsend[y, x]
    for copy in gather + forward + ask + answer + halves:
        copy.wait_send()
    for dy, dx in offsets[1:]:
        oy, ox = other(dy, dx)
        at = oy * nx + ox
        to(rsend.at[oy, ox], rrecv.at[at], rs_s.at[at], rs_r.at[at], {"vocab": twin}).wait_recv()
    total = rrecv[0].astype(f32)
    for k in range(1, chips):
        total = total + rrecv[k].astype(f32)
    gh[...] = total.astype(bf16)
    for copy in scatter:
        copy.wait_send()


def finish(gh, gw, gh_out, gw_out, sem):
    high = gw.shape[0] // PIECES
    copies = [
        pltpu.make_async_copy(gw.at[pl.ds(n * high, high)], gw_out.at[pl.ds(n * high, high)], sem.at[n])
        for n in range(PIECES)
    ]
    copies.append(pltpu.make_async_copy(gh, gh_out, sem.at[PIECES]))
    for copy in copies:
        copy.start()
    for copy in copies:
        copy.wait()


def per_device(nx, nz, hidden, head_weight, grad_pooled, lengths, argmax_local):
    tb, feats = hidden.shape
    terms = head_weight.shape[1]
    passages = lengths.shape[0]
    chips = lax.axis_size("vocab") // 2
    ny = chips // nx
    band = nx * tb
    tokens = 2 * ny * band
    share = terms // nz
    anywhere = pl.BlockSpec(memory_space=pl.ANY)
    dma = pltpu.SemaphoreType.DMA
    gh, gw = pl.pallas_call(
        functools.partial(kernel, ny, nx, nz),
        out_shape=(pltpu.VMEM((tb, feats), bf16), pltpu.VMEM((feats, terms), bf16)),
        in_specs=[anywhere] * 5,
        out_specs=(pl.BlockSpec(memory_space=pltpu.VMEM), pl.BlockSpec(memory_space=pltpu.VMEM)),
        scratch_shapes=[
            pltpu.VMEM((2, ny, nx, tb, feats), bf16),
            pltpu.VMEM((feats, tokens), bf16),
            pltpu.VMEM((feats, terms), bf16),
            pltpu.VMEM((terms, feats), bf16),
            pltpu.VMEM((2, ny, band, terms), bf16),
            pltpu.VMEM((2, ny, band, terms), bf16),
            pltpu.VMEM((passages, terms), jnp.int32),
            pltpu.VMEM((passages, share), f32),
            pltpu.VMEM((2, ny, band, passages), bf16),
            pltpu.VMEM((2, ny, passages, band), bf16),
            pltpu.VMEM((nz, passages, share), f32),
            pltpu.VMEM((nz, passages, share), bf16),
            pltpu.VMEM((nz, passages, share), bf16),
            pltpu.VMEM((nz, passages, share), bf16),
            pltpu.VMEM((ny, band, feats), bf16),
            pltpu.VMEM((ny, band, feats), bf16),
            pltpu.VMEM((ny, nx, tb, feats), bf16),
            pltpu.VMEM((chips, tb, feats), bf16),
            pltpu.SMEM((passages,), jnp.int32),
            dma((5,)),
            dma((chips,)), dma((chips,)),
            dma((ny,)), dma((ny,)),
            dma((nz,)), dma((nz,)),
            dma((nz,)), dma((nz,)),
            dma((ny,)), dma((ny,)),
            dma((chips,)), dma((chips,)),
        ],
        compiler_params=pltpu.CompilerParams(
            collective_id=0, has_side_effects=True, vmem_limit_bytes=56 * 1024 * 1024
        ),
        cost_estimate=pl.CostEstimate(
            flops=6 * tokens * feats * terms, bytes_accessed=4 * feats * terms, transcendentals=0
        ),
    )(lengths, hidden, head_weight, grad_pooled, argmax_local)
    return pl.pallas_call(
        finish,
        out_shape=(
            jax.ShapeDtypeStruct((tb, feats), bf16),
            jax.ShapeDtypeStruct((feats, terms), bf16),
        ),
        in_specs=[anywhere] * 2,
        out_specs=(anywhere, anywhere),
        scratch_shapes=[dma((PIECES + 1,))],
        compiler_params=pltpu.CompilerParams(vmem_limit_bytes=1024 * 1024),
    )(gh, gw)


def solution(mesh):
    in_specs = (P("vocab", "dp"), P("dp", "vocab"), P(None, "vocab"), P(), P(None, "vocab"))
    out_specs = (P("vocab", "dp"), P("dp", "vocab"))
    nx = 4 if mesh.shape["vocab"] == 32 else 2
    return jax.shard_map(
        functools.partial(per_device, nx, mesh.shape["dp"]),
        mesh=mesh, in_specs=in_specs, out_specs=out_specs, check_vma=False,
    )
```
